128 devices in a mesh: team: 4 (over z_lo, core), row: 32 (over x, z_hi, y).
Axes of the slice: x: 4, y: 4, z: 4 (z_hi: 2, z_lo: 2; z = z_hi * 2 + z_lo), core: 2. Of those that a mesh axis runs over, the one named last changes fastest.
Arguments:
- features: bfloat16 [65536, 128], P(('team', 'row')), may hold values from -6 to 6
- tile_values: bfloat16 [512, 12, 256, 256], P(('team', 'row')), may hold values from 0 to 0.09375, as said below
- tile_row: int32 [512, 12], P(('team', 'row')), may hold values from 0 to 1
- tile_col: int32 [512, 12], P(('team', 'row')), may hold values from 0 to 63
- tile_count: int32 [512], P(('team', 'row')), may hold values from 1 to 12, as said below
- weight: bfloat16 [128, 256], replicated, may hold values from -0.5 to 0.5
- bias: float32 [256], replicated, may hold values from -1.5 to 1.5
- cotangent: bfloat16 [65536, 256], P(('team', 'row')), may hold values from -0.0234375 to 0.0234375
Outputs:
- hidden: bfloat16 [65536, 256], P(('team', 'row'))
- weight_grad: float32 [128, 256], replicated
- bias_grad: float32 [256], replicated
The draws below stay inside these ranges and needn't reach their ends.
Inputs may be any that keep to these rules, and one draw needn't show every extreme that they name: Live tiles stand in the first tile_count[g] slots of group g. In every draw some owner has 12 live tiles in each of its 4 groups. `tile_values`: every entry is a whole multiple of 1 / 32; most entries are zero.
All inputs are finite; a program needn't handle non-finite values.
Results may differ from the reference program's by a relative error of at most 0.0052.
Values may be sent and summed in bfloat16 or wider, within the bound.
No kernel may reach another device: no remote copies, remote signals or barrier semaphores. Data moves between devices by JAX's collectives and lax.ppermute only.
A program may use at most 128 MiB of HBM per device.

```python
import jax
import jax.numpy as jnp
from jax import lax

FIN = 128
FOUT = 256
BLK = 256
ROW_BLOCKS = 2
SLOTS = 12
NODES = 65536
N_TEAM = 4
N_ROW = 32
DEVICES = 128


def draw_tile_values(key, part):
    key = jax.random.fold_in(key, 5)
    key_mask, key_level = jax.random.split(key, 2)
    shape = (DEVICES * N_TEAM, SLOTS, BLK, BLK)
    present = jax.random.randint(key_mask, shape, 0, 64) == 0
    levels = jax.random.randint(key_level, shape, 1, 4)
    return (jnp.where(present, levels, 0).astype(jnp.float32) * (1.0 / 32.0)).astype(jnp.bfloat16)


def draw_tile_count(key, part):
    key = jax.random.fold_in(key, 11)
    key_base, key_hot, key_forced = jax.random.split(key, 3)
    base = jax.random.randint(key_base, (DEVICES * N_TEAM,), 1, SLOTS // 2 + 1)
    hot_draw = jax.random.randint(key_hot, (DEVICES,), 0, 16) == 0
    forced = jax.random.randint(key_forced, (), 0, DEVICES)
    hot_owner = hot_draw | (jnp.arange(DEVICES) == forced)
    hot_group = jnp.repeat(hot_owner, N_TEAM)
    return jnp.where(hot_group, SLOTS, base).astype(jnp.int32)


def plant(array, key, least, largest):
    dims = array.shape
    spot = [jax.random.randint(jax.random.fold_in(key, axis), (), 0, dims[axis]) for axis in range(len(dims))]
    array = array.at[tuple(spot)].set(least)
    longest = dims.index(max(dims))
    spot[longest] = (spot[longest] + 1) % dims[longest]
    return array.at[tuple(spot)].set(largest)


def steps_of(rng, dims, pieces, smallest, top_value):
    gain, own = 1.0, jax.random.fold_in(rng, 6)
    for position, parts in pieces:
        heights = jnp.exp(jax.random.uniform(jax.random.fold_in(own, position), (parts,), jnp.float32, smallest / len(pieces), top_value / len(pieces)))
        gain = gain * jnp.repeat(heights, dims[position] // parts).reshape([-1 if axis == position else 1 for axis in range(len(dims))])
    return gain


def scatter_about(rng, shape, spread, reach, shards=(), kind=jnp.bfloat16):
    drawn = jax.random.normal(rng, shape, jnp.float32) * spread
    if len(shards) > 0:
        drawn = steps_of(rng, shape, shards, -0.22, 0.18) * drawn
    return jnp.clip(drawn, min=-reach, max=reach).astype(kind)


def setup_inputs(seed: int = 0) -> dict:
    keys = jax.random.split(jax.random.key(seed), 9)
    features = scatter_about(keys[0], (NODES, FIN), 1.0, 6.0, ((0, 128),))
    tile_values = draw_tile_values(jax.random.fold_in(keys[8], 71), 0)
    tile_row = plant(jax.random.randint(keys[2], (DEVICES * N_TEAM, SLOTS), 0, ROW_BLOCKS), jax.random.fold_in(keys[2], 1), 0, ROW_BLOCKS - 1).astype(jnp.int32)
    tile_col = plant(jax.random.randint(keys[3], (DEVICES * N_TEAM, SLOTS), 0, N_ROW * ROW_BLOCKS), jax.random.fold_in(keys[3], 1), 0, (N_ROW * ROW_BLOCKS) - 1).astype(jnp.int32)
    tile_count = draw_tile_count(jax.random.fold_in(keys[8], 71), 0)
    weight = scatter_about(keys[5], (FIN, FOUT), FIN ** -0.5, 0.5)
    bias = scatter_about(keys[6], (FOUT,), 0.25, 1.5, (), jnp.float32)
    cotangent = scatter_about(keys[7], (NODES, FOUT), NODES ** -0.5, 0.0234375, ((0, 128),))
    return {"features": features, "tile_values": tile_values, "tile_row": tile_row, "tile_col": tile_col, "tile_count": tile_count, "weight": weight, "bias": bias, "cotangent": cotangent}


def gelu_parts(values):
    gelu_coef = 0.7978845608
    tangent_h = jnp.tanh(gelu_coef * (values + 0.044715 * values * values * values))
    result = 0.5 * values * (1.0 + tangent_h)
    derive = 0.5 * (1.0 + tangent_h) + 0.5 * values * (1.0 - tangent_h * tangent_h) * gelu_coef * (1.0 + 3.0 * 0.044715 * values * values)
    return result, derive


def reference(features, tile_values, tile_row, tile_col, tile_count, weight, bias, cotangent):
    groups = tile_count.shape[0]
    owners = groups // N_TEAM
    block_feats = features.reshape(-1, BLK, FIN).astype(jnp.float32)
    panel_blocks = N_ROW * ROW_BLOCKS
    slot_ids = jnp.arange(SLOTS, dtype=jnp.int32)
    block_ids = jnp.arange(ROW_BLOCKS, dtype=jnp.int32)

    def add_group(total, group_id):
        owner = (group_id // N_TEAM).astype(jnp.int32)
        column_team = (group_id % N_TEAM).astype(jnp.int32)
        tiles = lax.dynamic_index_in_dim(tile_values, group_id, 0, False).astype(jnp.float32)
        col_index = column_team * panel_blocks + lax.dynamic_index_in_dim(tile_col, group_id, 0, False)
        row_index = lax.dynamic_index_in_dim(tile_row, group_id, 0, False)
        count = lax.dynamic_index_in_dim(tile_count, group_id, 0, False)
        picked = jnp.take(block_feats, col_index.astype(jnp.int32), axis=0)
        products = jnp.einsum("sij,sjf->sif", tiles, picked, precision=lax.Precision.HIGHEST)
        live_mask = slot_ids < count
        row_select = ((row_index[None, :] == block_ids[:, None]) & live_mask[None, :]).astype(jnp.float32)
        summed = jnp.einsum("rs,sif->rif", row_select, products, precision=lax.Precision.HIGHEST)
        start = (owner * ROW_BLOCKS).astype(jnp.int32)
        current = lax.dynamic_slice_in_dim(total, start, ROW_BLOCKS, 0)
        total = lax.dynamic_update_slice_in_dim(total, current + summed, start, 0)
        return total, None

    empty = jnp.zeros((owners * ROW_BLOCKS, BLK, FIN), jnp.float32)
    total, unused = lax.scan(add_group, empty, jnp.arange(groups, dtype=jnp.int32))
    aggregated = total.reshape(-1, FIN).astype(jnp.bfloat16)
    pre = jnp.dot(aggregated, weight, preferred_element_type=jnp.float32) + bias
    result, derive = gelu_parts(pre)
    hidden = result.astype(jnp.bfloat16)
    slope = cotangent.astype(jnp.float32) * derive
    slope_half = slope.astype(jnp.bfloat16)
    weight_grad = lax.dot_general(aggregated, slope_half, (((0,), (0,)), ((), ())), preferred_element_type=jnp.float32)
    bias_grad = jnp.sum(slope, axis=0)
    return hidden, weight_grad, bias_grad
```

```python
import functools

import jax
import jax.numpy as jnp
from jax import lax
from jax.experimental import pallas as pl
from jax.experimental.pallas import tpu as pltpu
from jax.sharding import Mesh, PartitionSpec as P

AXES = ("zlo", "core", "x", "zhi", "y")
AXIS_SIZES = (2, 2, 4, 2, 4)
PLANE = ("x", "y")
PEERS = 16


def z_of(index):
    return (index % 2) * 2 + index // 2


def ring(value, axis, step):
    if axis == "z":
        pairs = [(i, z_of((z_of(i) + step) % 4)) for i in range(4)]
        return lax.ppermute(value, ("zlo", "zhi"), pairs)
    size = lax.axis_size(axis)
    return lax.ppermute(value, axis, [(i, (i + step) % size) for i in range(size)])


def gather_kernel(need_ref, own_ref, one_ref, two_ref, three_ref, other_ref, out_ref, table_ref):
    part = own_ref.shape[0]
    for at, piece in enumerate((own_ref, one_ref, two_ref, three_ref)):
        table_ref[at * part : (at + 1) * part] = piece[...]
    table_ref[4 * part :] = other_ref[...]
    slots = out_ref.shape[1]

    def one_peer(peer, carry):
        for slot in range(slots):
            out_ref[peer, slot] = table_ref[need_ref[peer, slot]]
        return carry

    lax.fori_loop(0, out_ref.shape[0], one_peer, 0)


def gather_slices(need, own, one, two, three, other, slots):
    part, height, width = own.shape
    vmem = pl.BlockSpec(memory_space=pltpu.VMEM)
    return pl.pallas_call(
        gather_kernel,
        out_shape=jax.ShapeDtypeStruct((PEERS, slots, height, width), own.dtype),
        grid_spec=pltpu.PrefetchScalarGridSpec(
            num_scalar_prefetch=1,
            grid=(),
            in_specs=[vmem] * 5,
            out_specs=vmem,
            scratch_shapes=[pltpu.VMEM((8 * part, height, width), own.dtype)],
        ),
        compiler_params=pltpu.CompilerParams(vmem_limit_bytes=24 * 1024 * 1024),
        name="pick_slices",
    )(need, own, one, two, three, other)


def gelu_parts(values):
    gelu_coef = 0.7978845608
    tangent_h = jnp.tanh(gelu_coef * (values + 0.044715 * values * values * values))
    result = 0.5 * values * (1.0 + tangent_h)
    derive = 0.5 * (1.0 + tangent_h) + 0.5 * values * (1.0 - tangent_h * tangent_h) * gelu_coef * (
        1.0 + 3.0 * 0.044715 * values * values
    )
    return (result, derive)


def layer_kernel(
    row_ref, count_ref, tiles_ref, slices_ref, weight_ref, bias_ref, cotangent_ref, hidden_ref, grad_ref, total_ref
):
    group = pl.program_id(0)
    slots, block = tiles_ref.shape[1], tiles_ref.shape[2]

    @pl.when(group == 0)
    def _():
        total_ref[...] = jnp.zeros_like(total_ref)

    count = count_ref[group]
    for slot in range(slots):

        @pl.when(slot < count)
        def _():
            picked = jnp.concatenate([slices_ref[i, slot] for i in range(PEERS)], axis=0)
            product = jnp.dot(tiles_ref[0, slot], picked, preferred_element_type=jnp.float32)
            rows = pl.ds(pl.multiple_of(row_ref[group, slot] * block, block), block)
            total_ref[rows, :] += product

    @pl.when(group == pl.num_programs(0) - 1)
    def _():
        aggregated = total_ref[...].astype(jnp.bfloat16)
        pre = jnp.dot(aggregated, weight_ref[...], preferred_element_type=jnp.float32) + bias_ref[...]
        result, derive = gelu_parts(pre)
        hidden_ref[...] = result.astype(jnp.bfloat16)
        slope = cotangent_ref[...].astype(jnp.float32) * derive
        weight_part = lax.dot_general(
            aggregated,
            slope.astype(jnp.bfloat16),
            (((0,), (0,)), ((), ())),
            preferred_element_type=jnp.float32,
        )
        bias_part = jnp.sum(slope, axis=0, keepdims=True)
        grad_ref[:, :16, :] = weight_part.reshape(8, 16, weight_part.shape[1])
        first = lax.broadcasted_iota(jnp.int32, (8, bias_part.shape[1]), 0) == 0
        grad_ref[:, 16:, :] = jnp.zeros((8, 8, bias_part.shape[1]), jnp.float32)
        grad_ref[0, 16:, :] = jnp.where(first, bias_part, 0.0)


def layer(rows, counts, tiles, slices, weight, bias, cotangent):
    groups, slots, block, _ = tiles.shape
    nodes, out_width = cotangent.shape
    height, width = slices.shape[2:]
    whole = lambda shape: pl.BlockSpec(shape, lambda g, *_: (0,) * len(shape))
    return pl.pallas_call(
        layer_kernel,
        out_shape=(
            jax.ShapeDtypeStruct((nodes, out_width), jnp.bfloat16),
            jax.ShapeDtypeStruct((8, 24, out_width), jnp.float32),
        ),
        grid_spec=pltpu.PrefetchScalarGridSpec(
            num_scalar_prefetch=2,
            grid=(groups,),
            in_specs=[
                pl.BlockSpec((1, slots, block, block), lambda g, *_: (g, 0, 0, 0)),
                pl.BlockSpec((PEERS, slots, height, width), lambda g, *_: (0, g, 0, 0)),
                whole(weight.shape),
                whole((1, out_width)),
                whole(cotangent.shape),
            ],
            out_specs=(whole((nodes, out_width)), whole((8, 24, out_width))),
            scratch_shapes=[pltpu.VMEM((nodes, width), jnp.float32)],
        ),
        compiler_params=pltpu.CompilerParams(
            dimension_semantics=("arbitrary",), vmem_limit_bytes=32 * 1024 * 1024
        ),
        name="layer",
    )(rows, counts, tiles, slices, weight, bias.reshape(1, -1), cotangent)


def exchange(value, axis):
    one, two, three = (ring(value, axis, step) for step in (1, 2, 3))
    return (value + two) + (one + three)


def pick(stack, index):
    return lax.dynamic_index_in_dim(stack, index, 0, False)


def sum_over_devices(grad):
    core = lax.axis_index("core")
    depth = lax.axis_index("zhi") * 2 + lax.axis_index("zlo")
    halves = grad.reshape((2, 4) + grad.shape[1:])
    half = pick(halves, core) + ring(pick(halves, 1 - core), "core", 1)
    quarter = pick(half, depth)
    for step in (1, 2, 3):
        quarter = quarter + ring(pick(half, (depth + step) % 4), "z", step)
    quarter = exchange(quarter, "x")
    quarter = exchange(quarter, "y")
    stack = jnp.stack([quarter] + [ring(quarter, "z", step) for step in (1, 2, 3)])
    other = ring(stack, "core", 1)
    first, second = jnp.where(core == 0, stack, other), jnp.where(core == 0, other, stack)
    order = (depth - jnp.arange(4)) % 4
    both = jnp.stack([first, second])
    return jnp.take(both, order, axis=1).reshape(grad.shape)


def local(features, tile_values, tile_row, tile_col, tile_count, weight, bias, cotangent):
    groups, slots, block, _ = tile_values.shape
    width = features.shape[1]
    height = block // PEERS
    needed = groups * slots
    core = lax.axis_index("core")
    depth = lax.axis_index("zhi") * 2 + lax.axis_index("zlo")

    team = lax.broadcasted_iota(jnp.int32, (groups, slots), 0)
    holder, part = tile_col // 2, tile_col % 2
    there = ((holder // 4) % 2) * 2 + team // 2
    place = ((holder // 8) * 4 + holder % 4) * 2 + part
    turn = (team % 2) ^ core
    need = ((turn * 4 + (there - depth) % 4) * (2 * PEERS) + place).astype(jnp.bfloat16).reshape(1, needed)
    need = jnp.broadcast_to(jnp.pad(need, ((0, 0), (0, width - needed))), (height, width))

    mine = features.reshape(-1, PEERS, height, width).transpose(1, 0, 2, 3)
    lists = jnp.broadcast_to(need[None, None], (PEERS, 1, height, width))
    dealt = lax.all_to_all(jnp.concatenate([mine, lists], axis=1), PLANE, 0, 0)
    own = dealt[:, :2].reshape(2 * PEERS, height, width)
    wanted = dealt[:, 2, 0, :needed].astype(jnp.int32)

    one, two, three = (ring(own, "z", -step) for step in (1, 2, 3))
    other = ring(jnp.concatenate([own, one, two, three], axis=0), "core", 1)

    picked = gather_slices(wanted, own, one, two, three, other, needed)
    slices = lax.all_to_all(picked, PLANE, 0, 0)

    hidden, grad = layer(tile_row, tile_count, tile_values, slices, weight, bias, cotangent)
    summed = sum_over_devices(grad)
    weight_grad = summed[:, :16].reshape(weight.shape)
    return (hidden, weight_grad, summed[0, 16])


def solution(mesh):
    fine = Mesh(mesh.devices.reshape(AXIS_SIZES), AXES)
    nodes = P(AXES)
    in_specs = (nodes, nodes, nodes, nodes, nodes, P(), P(), nodes)
    return jax.shard_map(
        local, mesh=fine, in_specs=in_specs, out_specs=(nodes, P(), P()), check_vma=False
    )
```

```python
import jax
import jax.numpy as jnp
from jax import lax
from jax.experimental import pallas as pl
from jax.experimental.pallas import tpu as pltpu
from jax.sharding import Mesh, PartitionSpec as P

AXES = ("zlo", "core", "x", "zhi", "y")
AXIS_SIZES = (2, 2, 4, 2, 4)
PLANE = ("x", "y")
PEERS = 16


def z_of(index):
    return (index % 2) * 2 + index // 2


def ring(value, axis, step):
    if axis == "z":
        pairs = [(i, z_of((z_of(i) + step) % 4)) for i in range(4)]
        return lax.ppermute(value, ("zlo", "zhi"), pairs)
    size = lax.axis_size(axis)
    return lax.ppermute(value, axis, [(i, (i + step) % size) for i in range(size)])


def gather_kernel(need_ref, own_ref, one_ref, two_ref, three_ref, other_ref, out_ref, table_ref, stage_ref, sent):
    part = own_ref.shape[0]
    for at, piece in enumerate((own_ref, one_ref, two_ref, three_ref)):
        table_ref[at * part : (at + 1) * part] = piece[...]
    table_ref[4 * part :] = other_ref[...]
    slots = out_ref.shape[1]

    def one_peer(peer, carry):
        for slot in range(slots):
            stage_ref[peer, slot] = table_ref[need_ref[peer, slot]]
        return carry

    copies = []
    for run in range(sent.shape[0]):
        span = PEERS // sent.shape[0]
        lax.fori_loop(run * span, (run + 1) * span, one_peer, 0)
        peers = pl.ds(run * span, span)
        copies.append(pltpu.make_async_copy(stage_ref.at[peers], out_ref.at[peers], sent.at[run]))
        copies[-1].start()
    for copy in copies:
        copy.wait()


def gather_slices(need, own, one, two, three, other, slots):
    part, height, width = own.shape
    vmem = pl.BlockSpec(memory_space=pltpu.VMEM)
    shape = (PEERS, slots, height, width)
    return pl.pallas_call(
        gather_kernel,
        out_shape=jax.ShapeDtypeStruct(shape, own.dtype),
        in_specs=[pl.BlockSpec(memory_space=pltpu.SMEM)] + [vmem] * 5,
        out_specs=pl.BlockSpec(memory_space=pltpu.HBM),
        scratch_shapes=[
            pltpu.VMEM((8 * part, height, width), own.dtype),
            pltpu.VMEM(shape, own.dtype),
            pltpu.SemaphoreType.DMA((4,)),
        ],
        compiler_params=pltpu.CompilerParams(vmem_limit_bytes=24 * 1024 * 1024),
        name="pick_slices",
    )(need, own, one, two, three, other)


def gelu_parts(values):
    gelu_coef = 0.7978845608
    tangent_h = jnp.tanh(gelu_coef * (values + 0.044715 * values * values * values))
    result = 0.5 * values * (1.0 + tangent_h)
    derive = 0.5 * (1.0 + tangent_h) + 0.5 * values * (1.0 - tangent_h * tangent_h) * gelu_coef * (
        1.0 + 3.0 * 0.044715 * values * values
    )
    return (result, derive)


def layer_kernel(
    row_ref, count_ref, tiles_ref, slices_ref, weight_ref, bias_ref, cotangent_ref, hidden_ref, grad_ref, held, landed
):
    groups, slots = held.shape[:2]
    runs = landed.shape[1]
    span = slots // runs
    copies = []
    for group in range(groups):
        for run in range(runs):
            part = pl.ds(run * span, span)
            copies.append(
                pltpu.make_async_copy(tiles_ref.at[group, part], held.at[group, part], landed.at[group, run])
            )
            copies[-1].start()

    def spread(group, slot):
        picked = jnp.concatenate([slices_ref[i, group * slots + slot] for i in range(PEERS)], axis=0)
        row = jnp.where(slot < count_ref[group], row_ref[group, slot], 2)
        none = jnp.zeros_like(picked)
        return jnp.concatenate([jnp.where(row == 0, picked, none), jnp.where(row == 1, picked, none)], axis=1)

    total = None
    for group in range(groups):
        for run in range(runs):
            copies[group * runs + run].wait()
            part = range(run * span, (run + 1) * span)
            tiles = jnp.concatenate([held[group, slot] for slot in part], axis=1)
            picked = jnp.concatenate([spread(group, slot) for slot in part], axis=0)
            product = jnp.dot(tiles, picked, preferred_element_type=jnp.float32)
            total = product if total is None else total + product

    width = total.shape[1] // 2
    aggregated = jnp.concatenate([total[:, :width], total[:, width:]], axis=0).astype(jnp.bfloat16)
    pre = jnp.dot(aggregated, weight_ref[...], preferred_element_type=jnp.float32) + bias_ref[...]
    result, derive = gelu_parts(pre)
    hidden_ref[...] = result.astype(jnp.bfloat16)
    slope = cotangent_ref[...].astype(jnp.float32) * derive
    outs = slope.shape[1]
    grad_ref[:, :outs] = lax.dot_general(
        aggregated, slope.astype(jnp.bfloat16), (((0,), (0,)), ((), ())), preferred_element_type=jnp.float32
    )
    bias_part = jnp.sum(slope, axis=0, keepdims=True)
    at = lax.broadcasted_iota(jnp.int32, (width, outs - width), 0)
    last = jnp.where(at == 1, bias_part[:, width:], 0.0)
    grad_ref[:, outs:] = jnp.where(at == 0, bias_part[:, :width], last)


def layer(rows, counts, tiles, slices, weight, bias, cotangent):
    nodes, out_width = cotangent.shape
    width = weight.shape[0]
    runs = 2
    vmem = pl.BlockSpec(memory_space=pltpu.VMEM)
    smem = pl.BlockSpec(memory_space=pltpu.SMEM)
    return pl.pallas_call(
        layer_kernel,
        out_shape=(
            jax.ShapeDtypeStruct((nodes, out_width), jnp.bfloat16),
            jax.ShapeDtypeStruct((width, out_width + width), jnp.float32),
        ),
        in_specs=[smem, smem, pl.BlockSpec(memory_space=pltpu.HBM), vmem, vmem, vmem, vmem],
        out_specs=(vmem, vmem),
        scratch_shapes=[
            pltpu.VMEM(tiles.shape, tiles.dtype),
            pltpu.SemaphoreType.DMA((tiles.shape[0], runs)),
        ],
        compiler_params=pltpu.CompilerParams(vmem_limit_bytes=32 * 1024 * 1024),
        name="layer",
    )(rows, counts, tiles, slices, weight, bias.reshape(1, -1), cotangent)


def sum_over_devices(grad):
    rows = grad.reshape(grad.shape[0], -1, 128)
    total = jnp.sum(lax.all_to_all(rows, AXES, 0, 0), axis=0)
    return lax.all_to_all(jnp.broadcast_to(total[None], rows.shape), AXES, 0, 0)


def local(features, tile_values, tile_row, tile_col, tile_count, weight, bias, cotangent):
    groups, slots, block, _ = tile_values.shape
    width = features.shape[1]
    height = block // PEERS
    needed = groups * slots
    core = lax.axis_index("core")
    depth = lax.axis_index("zhi") * 2 + lax.axis_index("zlo")

    team = lax.broadcasted_iota(jnp.int32, (groups, slots), 0)
    holder, part = tile_col // 2, tile_col % 2
    there = ((holder // 4) % 2) * 2 + team // 2
    place = ((holder // 8) * 4 + holder % 4) * 2 + part
    turn = (team % 2) ^ core
    need = ((turn * 4 + (there - depth) % 4) * (2 * PEERS) + place).astype(jnp.bfloat16).reshape(1, needed)
    need = jnp.broadcast_to(jnp.pad(need, ((0, 0), (0, width - needed))), (height, width))

    mine = features.reshape(-1, PEERS, height, width).transpose(1, 0, 2, 3)
    lists = jnp.broadcast_to(need[None, None], (PEERS, 1, height, width))
    dealt = lax.all_to_all(jnp.concatenate([mine, lists], axis=1), PLANE, 0, 0)
    own = dealt[:, :2].reshape(2 * PEERS, height, width)
    wanted = dealt[:, 2, 0, :needed].astype(jnp.int32)

    one, two, three = (ring(own, "z", -step) for step in (1, 2, 3))
    other = ring(jnp.concatenate([own, one, two, three], axis=0), "core", 1)

    picked = gather_slices(wanted, own, one, two, three, other, needed)
    slices = lax.all_to_all(picked, PLANE, 0, 0)

    hidden, grad = layer(tile_row, tile_count, tile_values, slices, weight, bias, cotangent)
    summed = sum_over_devices(grad)
    return (hidden, summed[:, :2].reshape(weight.shape), summed[:2, 2].reshape(bias.shape))


def solution(mesh):
    fine = Mesh(mesh.devices.reshape(AXIS_SIZES), AXES)
    nodes = P(AXES)
    in_specs = (nodes, nodes, nodes, nodes, nodes, P(), P(), nodes)
    return jax.shard_map(
        local, mesh=fine, in_specs=in_specs, out_specs=(nodes, P(), P()), check_vma=False
    )
```

```python
import jax
import jax.numpy as jnp
from jax import lax
from jax.experimental import pallas as pl
from jax.experimental.pallas import tpu as pltpu
from jax.sharding import Mesh, PartitionSpec as P

AXES = ("zlo", "core", "x", "zhi", "y")
AXIS_SIZES = (2, 2, 4, 2, 4)
CHIPS = ("zlo", "x", "zhi", "y")
PEERS = 64
LANES = 128


def pick_kernel(need_ref, own_ref, other_ref, out_ref, stage_ref, sent):
    table = jnp.concatenate([own_ref[...], other_ref[...]], axis=0)
    need = need_ref[...]
    slots, runs = need.shape[0], sent.shape[0]
    span = PEERS // runs
    blocks = lax.broadcasted_iota(jnp.int32, (slots, table.shape[0]), 1)
    copies = []
    for run in range(runs):
        hot = [
            jnp.where(blocks == need[:, peer : peer + 1], 1.0, 0.0).astype(table.dtype)
            for peer in range(run * span, (run + 1) * span)
        ]
        rows = jnp.dot(jnp.concatenate(hot, axis=0), table, preferred_element_type=jnp.float32)
        stage_ref[run * span : (run + 1) * span] = rows.astype(table.dtype).reshape(span, slots, table.shape[1])
        peers = pl.ds(run * span, span)
        copies.append(pltpu.make_async_copy(stage_ref.at[peers], out_ref.at[peers], sent.at[run]))
        copies[-1].start()
    for copy in copies:
        copy.wait()


def pick_slices(need, own, other):
    vmem = pl.BlockSpec(memory_space=pltpu.VMEM)
    shape = (PEERS, need.shape[0], own.shape[1])
    return pl.pallas_call(
        pick_kernel,
        out_shape=jax.ShapeDtypeStruct(shape, own.dtype),
        in_specs=[vmem] * 3,
        out_specs=pl.BlockSpec(memory_space=pltpu.HBM),
        scratch_shapes=[pltpu.VMEM(shape, own.dtype), pltpu.SemaphoreType.DMA((8,))],
        compiler_params=pltpu.CompilerParams(vmem_limit_bytes=32 * 1024 * 1024),
        name="pick_slices",
    )(need, own, other)


def gelu_parts(values):
    gelu_coef = 0.7978845608
    tangent_h = jnp.tanh(gelu_coef * (values + 0.044715 * values * values * values))
    result = 0.5 * values * (1.0 + tangent_h)
    derive = 0.5 * (1.0 + tangent_h) + 0.5 * values * (1.0 - tangent_h * tangent_h) * gelu_coef * (
        1.0 + 3.0 * 0.044715 * values * values
    )
    return (result, derive)


def layer_kernel(
    row_ref, count_ref, tiles_ref, slices_ref, weight_ref, bias_ref, cotangent_ref, hidden_ref, grad_ref, held, wide, landed
):
    groups, slots = held.shape[:2]
    runs = landed.shape[1]
    span = slots // runs
    copies = []
    for group in range(groups):
        for run in range(runs):
            part = pl.ds(run * span, span)
            copies.append(
                pltpu.make_async_copy(tiles_ref.at[group, part], held.at[group, part], landed.at[group, run])
            )
            copies[-1].start()

    needed, stride = groups * slots, wide.shape[1] // PEERS
    turns = wide.shape[0]
    for peer in range(PEERS):
        for turn in range(turns):
            lanes = slices_ref[peer, :, turn * LANES : (turn + 1) * LANES]
            wide[turn, peer * stride : peer * stride + needed, :] = lanes.astype(jnp.float32)

    def spread(group, slot):
        at = pl.ds(group * slots + slot, PEERS, stride=stride)
        picked = jnp.concatenate([wide[turn, at, :] for turn in range(turns)], axis=0).astype(slices_ref.dtype)
        row = jnp.where(slot < count_ref[group], row_ref[group, slot], 2)
        none = jnp.zeros_like(picked)
        return jnp.concatenate([jnp.where(row == 0, picked, none), jnp.where(row == 1, picked, none)], axis=1)

    total = None
    for group in range(groups):
        for run in range(runs):
            copies[group * runs + run].wait()
            part = range(run * span, (run + 1) * span)
            tiles = jnp.concatenate([held[group, slot] for slot in part], axis=1)
            picked = jnp.concatenate([spread(group, slot) for slot in part], axis=0)
            product = jnp.dot(tiles, picked, preferred_element_type=jnp.float32)
            total = product if total is None else total + product

    width = total.shape[1] // 2
    aggregated = jnp.concatenate([total[:, :width], total[:, width:]], axis=0).astype(jnp.bfloat16)
    pre = jnp.dot(aggregated, weight_ref[...], preferred_element_type=jnp.float32) + bias_ref[...]
    result, derive = gelu_parts(pre)
    hidden_ref[...] = result.astype(jnp.bfloat16)
    slope = cotangent_ref[...].astype(jnp.float32) * derive
    outs = slope.shape[1]
    grad_ref[:, :outs] = lax.dot_general(
        aggregated, slope.astype(jnp.bfloat16), (((0,), (0,)), ((), ())), preferred_element_type=jnp.float32
    )
    bias_part = jnp.sum(slope, axis=0, keepdims=True)
    at = lax.broadcasted_iota(jnp.int32, (width, outs - width), 0)
    last = jnp.where(at == 1, bias_part[:, width:], 0.0)
    grad_ref[:, outs:] = jnp.where(at == 0, bias_part[:, :width], last)


def layer(rows, counts, tiles, slices, weight, bias, cotangent):
    nodes, out_width = cotangent.shape
    width = weight.shape[0]
    runs = 2
    vmem = pl.BlockSpec(memory_space=pltpu.VMEM)
    smem = pl.BlockSpec(memory_space=pltpu.SMEM)
    return pl.pallas_call(
        layer_kernel,
        out_shape=(
            jax.ShapeDtypeStruct((nodes, out_width), jnp.bfloat16),
            jax.ShapeDtypeStruct((width, out_width + width), jnp.float32),
        ),
        in_specs=[smem, smem, pl.BlockSpec(memory_space=pltpu.HBM), vmem, vmem, vmem, vmem],
        out_specs=(vmem, vmem),
        scratch_shapes=[
            pltpu.VMEM(tiles.shape, tiles.dtype),
            pltpu.VMEM((slices.shape[2] // LANES, PEERS * (slices.shape[1] + 1), LANES), jnp.float32),
            pltpu.SemaphoreType.DMA((tiles.shape[0], runs)),
        ],
        compiler_params=pltpu.CompilerParams(vmem_limit_bytes=40 * 1024 * 1024),
        name="layer",
    )(rows, counts, tiles, slices, weight, bias.reshape(1, -1), cotangent)


def sum_over_devices(grad):
    rows = grad.reshape(grad.shape[0], -1, 128)
    total = jnp.sum(lax.all_to_all(rows, AXES, 0, 0), axis=0)
    return lax.all_to_all(jnp.broadcast_to(total[None], rows.shape), AXES, 0, 0)


def local(features, tile_values, tile_row, tile_col, tile_count, weight, bias, cotangent):
    groups, slots, block, _ = tile_values.shape
    width = features.shape[1]
    turns = block // PEERS
    needed = groups * slots

    team = lax.broadcasted_iota(jnp.int32, (groups, slots), 0)
    need = ((team % 2) ^ lax.axis_index("core")) * (2 * PEERS) + (team // 2) * PEERS + tile_col
    need = jnp.pad(need.astype(jnp.bfloat16).reshape(needed), (0, width - needed))

    mine = features.reshape(-1, turns, PEERS, width).transpose(2, 0, 1, 3).reshape(PEERS, -1, turns * width)
    lists = jnp.broadcast_to(need, (PEERS, mine.shape[1], width))
    dealt = lax.all_to_all(jnp.concatenate([mine, lists], axis=2), CHIPS, 0, 0)
    own = dealt[:, :, : turns * width].reshape(-1, turns * width)
    wanted = dealt[:, 0, turns * width : turns * width + needed].astype(jnp.int32).T
    other = lax.ppermute(own, "core", [(0, 1), (1, 0)])

    slices = lax.all_to_all(pick_slices(wanted, own, other), CHIPS, 0, 0)

    hidden, grad = layer(tile_row, tile_count, tile_values, slices, weight, bias, cotangent)
    summed = sum_over_devices(grad)
    return (hidden, summed[:, :2].reshape(weight.shape), summed[:2, 2].reshape(bias.shape))


def solution(mesh):
    fine = Mesh(mesh.devices.reshape(AXIS_SIZES), AXES)
    nodes = P(AXES)
    in_specs = (nodes, nodes, nodes, nodes, nodes, P(), P(), nodes)
    return jax.shard_map(
        local, mesh=fine, in_specs=in_specs, out_specs=(nodes, P(), P()), check_vma=False
    )
```

```python
import math

import jax
import jax.numpy as jnp
from jax import lax
from jax.experimental import pallas as pl
from jax.experimental.pallas import tpu as pltpu
from jax.sharding import Mesh, PartitionSpec as P

AXES = ("zlo", "core", "x", "zhi", "y")
AXIS_SIZES = (2, 2, 4, 2, 4)
CHIPS = ("zlo", "x", "zhi", "y")
SIZE = dict(zip(AXES, AXIS_SIZES))
ALIKE = ("zhi",)
DEAL = tuple(axis for axis in CHIPS if axis not in ALIKE)
PEERS = math.prod(SIZE[axis] for axis in DEAL)
SPAN = 8
RUN = 6
LANES = 128


def pick_kernel(need_ref, own_ref, other_ref, out_ref):
    table = jnp.concatenate([own_ref[...], other_ref[...]], axis=0)
    need = need_ref[...]
    slots, span = need.shape[0], SPAN
    blocks = lax.broadcasted_iota(jnp.int32, (slots, table.shape[0]), 1)
    for run in range(PEERS // span):
        hot = [
            jnp.where(blocks == need[:, peer : peer + 1], 1.0, 0.0).astype(table.dtype)
            for peer in range(run * span, (run + 1) * span)
        ]
        rows = jnp.dot(jnp.concatenate(hot, axis=0), table, preferred_element_type=jnp.float32)
        out_ref[run * span : (run + 1) * span] = rows.astype(table.dtype).reshape(span, slots, table.shape[1])


def pick_slices(need, own, other):
    vmem = pl.BlockSpec(memory_space=pltpu.VMEM)
    shape = (PEERS, need.shape[0], own.shape[1])
    return pl.pallas_call(
        pick_kernel,
        out_shape=jax.ShapeDtypeStruct(shape, own.dtype),
        in_specs=[vmem] * 3,
        out_specs=vmem,
        compiler_params=pltpu.CompilerParams(vmem_limit_bytes=32 * 1024 * 1024),
        name="pick_slices",
    )(need, own, other)


def gelu_parts(values):
    gelu_coef = 0.7978845608
    tangent_h = jnp.tanh(gelu_coef * (values + 0.044715 * values * values * values))
    result = 0.5 * values * (1.0 + tangent_h)
    derive = 0.5 * (1.0 + tangent_h) + 0.5 * values * (1.0 - tangent_h * tangent_h) * gelu_coef * (
        1.0 + 3.0 * 0.044715 * values * values
    )
    return (result, derive)


def layer_kernel(
    row_ref, count_ref, tiles_ref, slices_ref, weight_ref, bias_ref, cotangent_ref, hidden_ref, grad_ref, wide
):
    groups, slots = tiles_ref.shape[:2]

    needed, stride = groups * slots, wide.shape[1] // PEERS
    turns = wide.shape[0]
    for peer in range(PEERS):
        for turn in range(turns):
            lanes = slices_ref[peer, :, turn * LANES : (turn + 1) * LANES]
            wide[turn, peer * stride : peer * stride + needed, :] = lanes.astype(jnp.float32)

    def spread(group, slot):
        at = pl.ds(group * slots + slot, PEERS, stride=stride)
        picked = jnp.concatenate([wide[turn, at, :] for turn in range(turns)], axis=0).astype(slices_ref.dtype)
        row = jnp.where(slot < count_ref[group], row_ref[group, slot], 2)
        none = jnp.zeros_like(picked)
        return jnp.concatenate([jnp.where(row == 0, picked, none), jnp.where(row == 1, picked, none)], axis=1)

    total = None
    for group in range(groups):
        for first in range(0, slots, RUN):
            run = range(first, first + RUN)
            tiles = jnp.concatenate([tiles_ref[group, slot] for slot in run], axis=1)
            picked = jnp.concatenate([spread(group, slot) for slot in run], axis=0)
            product = jnp.dot(tiles, picked, preferred_element_type=jnp.float32)
            total = product if total is None else total + product

    width = total.shape[1] // 2
    aggregated = jnp.concatenate([total[:, :width], total[:, width:]], axis=0).astype(jnp.bfloat16)
    pre = jnp.dot(aggregated, weight_ref[...], preferred_element_type=jnp.float32) + bias_ref[...]
    result, derive = gelu_parts(pre)
    hidden_ref[...] = result.astype(jnp.bfloat16)
    slope = cotangent_ref[...].astype(jnp.float32) * derive
    outs = slope.shape[1]
    grad_ref[:, :outs] = lax.dot_general(
        aggregated, slope.astype(jnp.bfloat16), (((0,), (0,)), ((), ())), preferred_element_type=jnp.float32
    )
    bias_part = jnp.sum(slope, axis=0, keepdims=True)
    at = lax.broadcasted_iota(jnp.int32, (width, outs - width), 0)
    last = jnp.where(at == 1, bias_part[:, width:], 0.0)
    grad_ref[:, outs:] = jnp.where(at == 0, bias_part[:, :width], last)


def layer(rows, counts, tiles, slices, weight, bias, cotangent):
    nodes, out_width = cotangent.shape
    width = weight.shape[0]
    vmem = pl.BlockSpec(memory_space=pltpu.VMEM)
    smem = pl.BlockSpec(memory_space=pltpu.SMEM)
    return pl.pallas_call(
        layer_kernel,
        out_shape=(
            jax.ShapeDtypeStruct((nodes, out_width), jnp.bfloat16),
            jax.ShapeDtypeStruct((width, out_width + width), jnp.float32),
        ),
        in_specs=[smem, smem, vmem, vmem, vmem, vmem, vmem],
        out_specs=(vmem, vmem),
        scratch_shapes=[
            pltpu.VMEM((slices.shape[2] // LANES, PEERS * (slices.shape[1] + 1), LANES), jnp.float32),
        ],
        compiler_params=pltpu.CompilerParams(vmem_limit_bytes=32 * 1024 * 1024),
        name="layer",
    )(rows, counts, tiles, slices, weight, bias.reshape(1, -1), cotangent)


def sum_over_devices(grad):
    rows = grad.reshape(grad.shape[0], -1, 128)
    total = jnp.sum(lax.all_to_all(rows, AXES, 0, 0), axis=0)
    return lax.all_to_all(jnp.broadcast_to(total[None], rows.shape), AXES, 0, 0)


def local(features, tile_values, tile_row, tile_col, tile_count, weight, bias, cotangent):
    groups, slots, block, _ = tile_values.shape
    width = features.shape[1]
    turns = block // PEERS
    needed = groups * slots

    chips = math.prod(SIZE[axis] for axis in CHIPS)
    team = lax.broadcasted_iota(jnp.int32, (groups, slots), 0)
    need = ((team % 2) ^ lax.axis_index("core")) * (2 * chips) + (team // 2) * chips + tile_col
    need = jnp.pad(need.astype(jnp.bfloat16).reshape(needed), (0, width - needed))

    mine = features.reshape(-1, turns, PEERS, width).transpose(2, 0, 1, 3).reshape(PEERS, -1, turns * width)
    mine = jnp.concatenate([mine, jnp.broadcast_to(need, (PEERS, mine.shape[1], width))], axis=2)
    grid = [SIZE[axis] for axis in CHIPS]
    once = [1 if axis in ALIKE else SIZE[axis] for axis in CHIPS]
    mine = jnp.broadcast_to(mine.reshape(once + list(mine.shape[1:])), grid + list(mine.shape[1:]))
    dealt = lax.all_to_all(mine.reshape((chips,) + mine.shape[len(grid) :]), CHIPS, 0, 0)
    own = dealt[:, :, : turns * width].reshape(-1, turns * width)
    lists = dealt[:, 0, turns * width : turns * width + needed].reshape(grid + [needed])
    for axis in ALIKE:
        lists = lax.dynamic_slice_in_dim(lists, lax.axis_index(axis), 1, CHIPS.index(axis))
    wanted = lists.reshape(PEERS, needed).astype(jnp.int32).T
    other = lax.ppermute(own, "core", [(0, 1), (1, 0)])

    slices = lax.all_to_all(pick_slices(wanted, own, other), DEAL, 0, 0)

    hidden, grad = layer(tile_row, tile_count, tile_values, slices, weight, bias, cotangent)
    summed = sum_over_devices(grad)
    return (hidden, summed[:, :2].reshape(weight.shape), summed[:2, 2].reshape(bias.shape))


def solution(mesh):
    fine = Mesh(mesh.devices.reshape(AXIS_SIZES), AXES)
    nodes = P(AXES)
    in_specs = (nodes, nodes, nodes, nodes, nodes, P(), P(), nodes)
    return jax.shard_map(
        local, mesh=fine, in_specs=in_specs, out_specs=(nodes, P(), P()), check_vma=False
    )
```

```python
import math

import jax
import jax.numpy as jnp
from jax import lax
from jax.experimental import pallas as pl
from jax.experimental.pallas import tpu as pltpu
from jax.sharding import Mesh, PartitionSpec as P

AXES = ("zlo", "core", "x", "zhi", "y")
AXIS_SIZES = (2, 2, 4, 2, 4)
SIZE = dict(zip(AXES, AXIS_SIZES))
ALIKE = ("zhi",)
DEAL = tuple(axis for axis in AXES if axis not in ALIKE)
PEERS = math.prod(SIZE[axis] for axis in DEAL)
SPAN = 8
RUN = 6
LANES = 128


def pick_kernel(need_ref, table_ref, out_ref):
    table = table_ref[...]
    need = need_ref[...]
    slots, span = need.shape[0], SPAN
    blocks = lax.broadcasted_iota(jnp.int32, (slots, table.shape[0]), 1)
    for run in range(PEERS // span):
        hot = [
            jnp.where(blocks == need[:, peer : peer + 1], 1.0, 0.0).astype(table.dtype)
            for peer in range(run * span, (run + 1) * span)
        ]
        rows = jnp.dot(jnp.concatenate(hot, axis=0), table, preferred_element_type=jnp.float32)
        out_ref[run * span : (run + 1) * span] = rows.astype(table.dtype).reshape(span, slots, table.shape[1])


def pick_slices(need, table):
    vmem = pl.BlockSpec(memory_space=pltpu.VMEM)
    shape = (PEERS, need.shape[0], table.shape[1])
    return pl.pallas_call(
        pick_kernel,
        out_shape=jax.ShapeDtypeStruct(shape, table.dtype),
        in_specs=[vmem] * 2,
        out_specs=vmem,
        compiler_params=pltpu.CompilerParams(vmem_limit_bytes=32 * 1024 * 1024),
        name="pick_slices",
    )(need, table)


def gelu_parts(values):
    gelu_coef = 0.7978845608
    tangent_h = jnp.tanh(gelu_coef * (values + 0.044715 * values * values * values))
    result = 0.5 * values * (1.0 + tangent_h)
    derive = 0.5 * (1.0 + tangent_h) + 0.5 * values * (1.0 - tangent_h * tangent_h) * gelu_coef * (
        1.0 + 3.0 * 0.044715 * values * values
    )
    return (result, derive)


def layer_kernel(
    row_ref, count_ref, tiles_ref, slices_ref, weight_ref, bias_ref, cotangent_ref, hidden_ref, grad_ref, wide
):
    groups, slots = tiles_ref.shape[:2]

    needed, stride = groups * slots, wide.shape[1] // PEERS
    turns = wide.shape[0]
    for peer in range(PEERS):
        for turn in range(turns):
            lanes = slices_ref[peer, :, turn * LANES : (turn + 1) * LANES]
            wide[turn, peer * stride : peer * stride + needed, :] = lanes.astype(jnp.float32)

    def spread(group, slot):
        at = pl.ds(group * slots + slot, PEERS, stride=stride)
        picked = jnp.concatenate([wide[turn, at, :] for turn in range(turns)], axis=0).astype(slices_ref.dtype)
        row = jnp.where(slot < count_ref[group], row_ref[group, slot], 2)
        none = jnp.zeros_like(picked)
        return jnp.concatenate([jnp.where(row == 0, picked, none), jnp.where(row == 1, picked, none)], axis=1)

    total = None
    for group in range(groups):
        for first in range(0, slots, RUN):
            run = range(first, first + RUN)
            tiles = jnp.concatenate([tiles_ref[group, slot] for slot in run], axis=1)
            picked = jnp.concatenate([spread(group, slot) for slot in run], axis=0)
            product = jnp.dot(tiles, picked, preferred_element_type=jnp.float32)
            total = product if total is None else total + product

    width = total.shape[1] // 2
    aggregated = jnp.concatenate([total[:, :width], total[:, width:]], axis=0).astype(jnp.bfloat16)
    pre = jnp.dot(aggregated, weight_ref[...], preferred_element_type=jnp.float32) + bias_ref[...]
    result, derive = gelu_parts(pre)
    hidden_ref[...] = result.astype(jnp.bfloat16)
    slope = cotangent_ref[...].astype(jnp.float32) * derive
    outs = slope.shape[1]
    grad_ref[:, :outs] = lax.dot_general(
        aggregated, slope.astype(jnp.bfloat16), (((0,), (0,)), ((), ())), preferred_element_type=jnp.float32
    )
    bias_part = jnp.sum(slope, axis=0, keepdims=True)
    at = lax.broadcasted_iota(jnp.int32, (width, outs - width), 0)
    last = jnp.where(at == 1, bias_part[:, width:], 0.0)
    grad_ref[:, outs:] = jnp.where(at == 0, bias_part[:, :width], last)


def layer(rows, counts, tiles, slices, weight, bias, cotangent):
    nodes, out_width = cotangent.shape
    width = weight.shape[0]
    vmem = pl.BlockSpec(memory_space=pltpu.VMEM)
    smem = pl.BlockSpec(memory_space=pltpu.SMEM)
    return pl.pallas_call(
        layer_kernel,
        out_shape=(
            jax.ShapeDtypeStruct((nodes, out_width), jnp.bfloat16),
            jax.ShapeDtypeStruct((width, out_width + width), jnp.float32),
        ),
        in_specs=[smem, smem, vmem, vmem, vmem, vmem, vmem],
        out_specs=(vmem, vmem),
        scratch_shapes=[
            pltpu.VMEM((slices.shape[2] // LANES, PEERS * (slices.shape[1] + 1), LANES), jnp.float32),
        ],
        compiler_params=pltpu.CompilerParams(vmem_limit_bytes=32 * 1024 * 1024),
        name="layer",
    )(rows, counts, tiles, slices, weight, bias.reshape(1, -1), cotangent)


def sum_over_devices(grad):
    group = ('zlo', 'core', 'x', 'zhi', 'y')
    size = math.prod(SIZE[axis] for axis in group)
    rows = grad.reshape(size, -1, grad.shape[1])
    total = jnp.sum(lax.all_to_all(rows, group, 0, 0), axis=0)
    shared = lax.all_to_all(jnp.broadcast_to(total[None], rows.shape), group, 0, 0)
    return shared.reshape(grad.shape)


def local(features, tile_values, tile_row, tile_col, tile_count, weight, bias, cotangent):
    groups, slots, block, _ = tile_values.shape
    width = features.shape[1]
    turns = block // PEERS
    needed = groups * slots

    team = lax.broadcasted_iota(jnp.int32, (groups, slots), 0)
    need = team * (2 * lax.axis_size(AXES) // groups) + tile_col
    need = jnp.pad(need.astype(jnp.bfloat16).reshape(needed), (0, width - needed))

    mine = features.reshape(-1, turns, PEERS, width).transpose(2, 0, 1, 3).reshape(PEERS, -1, turns * width)
    grid = [SIZE[axis] for axis in AXES]
    once = [1 if axis in ALIKE else SIZE[axis] for axis in AXES]
    copies = [SIZE[axis] if axis in ALIKE else 1 for axis in AXES]
    near = jnp.ones(copies + [1, 1], need.dtype)
    for axis in ALIKE:
        at = lax.broadcasted_iota(jnp.int32, near.shape, AXES.index(axis))
        near = jnp.where(at == lax.axis_index(axis), near, 0)
    rows = jnp.broadcast_to(mine.reshape(once + list(mine.shape[1:])), grid + list(mine.shape[1:]))
    lists = jnp.broadcast_to(need * near, grid + [mine.shape[1], width])
    sent = jnp.concatenate([rows, lists], axis=len(grid) + 1)
    dealt = lax.all_to_all(sent.reshape((-1,) + sent.shape[len(grid) :]), AXES, 0, 0)
    table = dealt[:, :, : turns * width].reshape(-1, turns * width)
    lists = dealt[:, 0, turns * width : turns * width + needed].reshape(grid + [needed])
    for axis in ALIKE:
        lists = jnp.max(lists, axis=AXES.index(axis), keepdims=True)
    wanted = lists.reshape(PEERS, needed).astype(jnp.int32).T

    slices = lax.all_to_all(pick_slices(wanted, table), DEAL, 0, 0)

    hidden, grad = layer(tile_row, tile_count, tile_values, slices, weight, bias, cotangent)
    summed = sum_over_devices(grad)
    return (hidden, summed[:, : bias.shape[0]], summed[:2, bias.shape[0] :].reshape(bias.shape))


def solution(mesh):
    fine = Mesh(mesh.devices.reshape(AXIS_SIZES), AXES)
    nodes = P(AXES)
    in_specs = (nodes, nodes, nodes, nodes, nodes, P(), P(), nodes)
    return jax.shard_map(
        local, mesh=fine, in_specs=in_specs, out_specs=(nodes, P(), P()), check_vma=False
    )
```

```python
import math

import jax
import jax.numpy as jnp
from jax import lax
from jax.experimental import pallas as pl
from jax.experimental.pallas import tpu as pltpu
from jax.sharding import Mesh, PartitionSpec as P

AXES = ("zlo", "core", "x", "zhi", "y")
AXIS_SIZES = (2, 2, 4, 2, 4)
SIZE = dict(zip(AXES, AXIS_SIZES))
ALIKE = ("zhi",)
DEAL = tuple(axis for axis in AXES if axis not in ALIKE)
PEERS = math.prod(SIZE[axis] for axis in DEAL)
SPAN = 8
RUN = 6
LANES = 128
PANEL = 2 * math.prod(AXIS_SIZES) // 4


def pick_kernel(need_ref, table_ref, out_ref):
    table = table_ref[...]
    need = need_ref[...]
    slots, span = need.shape[0], SPAN
    blocks = lax.broadcasted_iota(jnp.int32, (slots, table.shape[0]), 1)
    for run in range(PEERS // span):
        hot = [
            jnp.where(blocks == need[:, peer : peer + 1], 1.0, 0.0).astype(table.dtype)
            for peer in range(run * span, (run + 1) * span)
        ]
        rows = jnp.dot(jnp.concatenate(hot, axis=0), table, preferred_element_type=jnp.float32)
        out_ref[run * span : (run + 1) * span] = rows.astype(table.dtype).reshape(span, slots, table.shape[1])


def pick_slices(need, table):
    vmem = pl.BlockSpec(memory_space=pltpu.VMEM)
    shape = (PEERS, need.shape[0], table.shape[1])
    return pl.pallas_call(
        pick_kernel,
        out_shape=jax.ShapeDtypeStruct(shape, table.dtype),
        in_specs=[vmem] * 2,
        out_specs=vmem,
        compiler_params=pltpu.CompilerParams(vmem_limit_bytes=32 * 1024 * 1024),
        name="pick_slices",
    )(need, table)


def gelu_parts(values):
    gelu_coef = 0.7978845608
    tangent_h = jnp.tanh(gelu_coef * (values + 0.044715 * values * values * values))
    result = 0.5 * values * (1.0 + tangent_h)
    derive = 0.5 * (1.0 + tangent_h) + 0.5 * values * (1.0 - tangent_h * tangent_h) * gelu_coef * (
        1.0 + 3.0 * 0.044715 * values * values
    )
    return (result, derive)


def layer_kernel(
    row_ref, count_ref, tiles_ref, slices_ref, weight_ref, bias_ref, cotangent_ref, hidden_ref, grad_ref, wide
):
    groups, slots = tiles_ref.shape[:2]

    needed, stride = groups * slots, wide.shape[1] // PEERS
    turns = wide.shape[0]
    for peer in range(PEERS):
        for turn in range(turns):
            lanes = slices_ref[peer, :, turn * LANES : (turn + 1) * LANES]
            wide[turn, peer * stride : peer * stride + needed, :] = lanes.astype(jnp.float32)

    def spread(group, slot):
        at = pl.ds(group * slots + slot, PEERS, stride=stride)
        picked = jnp.concatenate([wide[turn, at, :] for turn in range(turns)], axis=0).astype(slices_ref.dtype)
        row = jnp.where(slot < count_ref[group], row_ref[group, slot], 2)
        none = jnp.zeros_like(picked)
        return jnp.concatenate([jnp.where(row == 0, picked, none), jnp.where(row == 1, picked, none)], axis=1)

    total = None
    for group in range(groups):
        for first in range(0, slots, RUN):
            run = range(first, first + RUN)
            tiles = jnp.concatenate([tiles_ref[group, slot] for slot in run], axis=1)
            picked = jnp.concatenate([spread(group, slot) for slot in run], axis=0)
            product = jnp.dot(tiles, picked, preferred_element_type=jnp.float32)
            total = product if total is None else total + product

    width = total.shape[1] // 2
    aggregated = jnp.concatenate([total[:, :width], total[:, width:]], axis=0).astype(jnp.bfloat16)
    pre = jnp.dot(aggregated, weight_ref[...], preferred_element_type=jnp.float32) + bias_ref[...]
    result, derive = gelu_parts(pre)
    hidden_ref[...] = result.astype(jnp.bfloat16)
    slope = cotangent_ref[...].astype(jnp.float32) * derive
    outs = slope.shape[1]
    grad_ref[:, :outs] = lax.dot_general(
        aggregated, slope.astype(jnp.bfloat16), (((0,), (0,)), ((), ())), preferred_element_type=jnp.float32
    )
    bias_part = jnp.sum(slope, axis=0, keepdims=True)
    at = lax.broadcasted_iota(jnp.int32, (width, outs - width), 0)
    last = jnp.where(at == 1, bias_part[:, width:], 0.0)
    grad_ref[:, outs:] = jnp.where(at == 0, bias_part[:, :width], last)


def layer(rows, counts, tiles, slices, weight, bias, cotangent):
    nodes, out_width = cotangent.shape
    width = weight.shape[0]
    vmem = pl.BlockSpec(memory_space=pltpu.VMEM)
    smem = pl.BlockSpec(memory_space=pltpu.SMEM)
    return pl.pallas_call(
        layer_kernel,
        out_shape=(
            jax.ShapeDtypeStruct((nodes, out_width), jnp.bfloat16),
            jax.ShapeDtypeStruct((width, out_width + width), jnp.float32),
        ),
        in_specs=[smem, smem, vmem, vmem, vmem, vmem, vmem],
        out_specs=(vmem, vmem),
        scratch_shapes=[
            pltpu.VMEM((slices.shape[2] // LANES, PEERS * (slices.shape[1] + 1), LANES), jnp.float32),
        ],
        compiler_params=pltpu.CompilerParams(vmem_limit_bytes=32 * 1024 * 1024),
        name="layer",
    )(rows, counts, tiles, slices, weight, bias.reshape(1, -1), cotangent)


def sum_over_devices(grad):
    group = ('zlo', 'core', 'x', 'zhi', 'y')
    size = math.prod(SIZE[axis] for axis in group)
    rows = grad.reshape(size, -1, grad.shape[1])
    total = jnp.sum(lax.all_to_all(rows, group, 0, 0), axis=0)
    shared = lax.all_to_all(jnp.broadcast_to(total[None], rows.shape), group, 0, 0)
    return shared.reshape(grad.shape)


def stage_kernel(features_ref, cols_ref, features_out, cols_out):
    features_out[...] = features_ref[...]
    groups, slots = cols_ref.shape
    team = lax.broadcasted_iota(jnp.int32, (groups, slots), 0)
    need = (team * PANEL + cols_ref[...]).astype(jnp.bfloat16)
    row = jnp.zeros((1, LANES), jnp.float32)
    for group in range(groups):
        at = lax.broadcasted_iota(jnp.int32, (slots, LANES), 1)
        own = lax.broadcasted_iota(jnp.int32, (slots, LANES), 0) + group * slots
        put = jnp.where(at == own, 1.0, 0.0).astype(jnp.bfloat16)
        row += jnp.dot(need[group : group + 1], put, preferred_element_type=jnp.float32)
    cols_out[...] = row.astype(jnp.bfloat16)


def stage(features, cols):
    vmem = pl.BlockSpec(memory_space=pltpu.VMEM)
    return pl.pallas_call(
        stage_kernel,
        out_shape=(
            pltpu.VMEM(features.shape, features.dtype),
            pltpu.VMEM((1, LANES), jnp.bfloat16),
        ),
        in_specs=[vmem, vmem],
        out_specs=(vmem, vmem),
        name="stage",
    )(features, cols)


def local(features, tile_values, tile_row, tile_col, tile_count, weight, bias, cotangent):
    groups, slots, block, _ = tile_values.shape
    width = features.shape[1]
    turns = block // PEERS
    needed = groups * slots

    features, need = stage(features, tile_col)
    need = need.reshape(width)

    mine = features.reshape(-1, turns, PEERS, width).transpose(2, 0, 1, 3).reshape(PEERS, -1, turns * width)
    grid = [SIZE[axis] for axis in AXES]
    once = [1 if axis in ALIKE else SIZE[axis] for axis in AXES]
    copies = [SIZE[axis] if axis in ALIKE else 1 for axis in AXES]
    near = jnp.ones(copies + [1, 1], need.dtype)
    for axis in ALIKE:
        at = lax.broadcasted_iota(jnp.int32, near.shape, AXES.index(axis))
        near = jnp.where(at == lax.axis_index(axis), near, 0)
    rows = jnp.broadcast_to(mine.reshape(once + list(mine.shape[1:])), grid + list(mine.shape[1:]))
    lists = jnp.broadcast_to(need * near, grid + [mine.shape[1], width])
    sent = jnp.concatenate([rows, lists], axis=len(grid) + 1)
    dealt = lax.all_to_all(sent.reshape((-1,) + sent.shape[len(grid) :]), AXES, 0, 0)
    table = dealt[:, :, : turns * width].reshape(-1, turns * width)
    lists = dealt[:, 0, turns * width : turns * width + needed].reshape(grid + [needed])
    for axis in ALIKE:
        lists = jnp.max(lists, axis=AXES.index(axis), keepdims=True)
    wanted = lists.reshape(PEERS, needed).astype(jnp.int32).T

    slices = lax.all_to_all(pick_slices(wanted, table), DEAL, 0, 0)

    hidden, grad = layer(tile_row, tile_count, tile_values, slices, weight, bias, cotangent)
    summed = sum_over_devices(grad)
    return (hidden, summed[:, : bias.shape[0]], summed[:2, bias.shape[0] :].reshape(bias.shape))


def solution(mesh):
    fine = Mesh(mesh.devices.reshape(AXIS_SIZES), AXES)
    nodes = P(AXES)
    in_specs = (nodes, nodes, nodes, nodes, nodes, P(), P(), nodes)
    return jax.shard_map(
        local, mesh=fine, in_specs=in_specs, out_specs=(nodes, P(), P()), check_vma=False
    )
```

```python
import math

import jax
import jax.numpy as jnp
from jax import lax
from jax.experimental import pallas as pl
from jax.experimental.pallas import tpu as pltpu
from jax.sharding import Mesh, PartitionSpec as P

AXES = ("zlo", "core", "x", "zhi", "y")
AXIS_SIZES = (2, 2, 4, 2, 4)
SIZE = dict(zip(AXES, AXIS_SIZES))
ALIKE = ("zhi",)
DEAL = tuple(axis for axis in AXES if axis not in ALIKE)
PEERS = math.prod(SIZE[axis] for axis in DEAL)
SPAN = 8
RUN = 6
LANES = 128
PANEL = 2 * math.prod(AXIS_SIZES) // 4


def pick_kernel(need_ref, table_ref, out_ref):
    table = table_ref[...]
    need = need_ref[...]
    slots, span = need.shape[0], SPAN
    blocks = lax.broadcasted_iota(jnp.int32, (slots, table.shape[0]), 1)
    for run in range(PEERS // span):
        hot = [
            jnp.where(blocks == need[:, peer : peer + 1], 1.0, 0.0).astype(table.dtype)
            for peer in range(run * span, (run + 1) * span)
        ]
        rows = jnp.dot(jnp.concatenate(hot, axis=0), table, preferred_element_type=jnp.float32)
        out_ref[run * span : (run + 1) * span] = rows.astype(table.dtype).reshape(span, slots, table.shape[1])


def pick_slices(need, table):
    vmem = pl.BlockSpec(memory_space=pltpu.VMEM)
    shape = (PEERS, need.shape[0], table.shape[1])
    return pl.pallas_call(
        pick_kernel,
        out_shape=jax.ShapeDtypeStruct(shape, table.dtype),
        in_specs=[vmem] * 2,
        out_specs=vmem,
        compiler_params=pltpu.CompilerParams(vmem_limit_bytes=32 * 1024 * 1024),
        name="pick_slices",
    )(need, table)


def gelu_parts(values):
    gelu_coef = 0.7978845608
    tangent_h = jnp.tanh(gelu_coef * (values + 0.044715 * values * values * values))
    result = 0.5 * values * (1.0 + tangent_h)
    derive = 0.5 * (1.0 + tangent_h) + 0.5 * values * (1.0 - tangent_h * tangent_h) * gelu_coef * (
        1.0 + 3.0 * 0.044715 * values * values
    )
    return (result, derive)


def layer_kernel(
    row_ref, count_ref, tiles_ref, slices_ref, weight_ref, bias_ref, cotangent_ref, hidden_ref, grad_ref, wide
):
    groups, slots = tiles_ref.shape[:2]

    needed, stride = groups * slots, wide.shape[1] // PEERS
    turns = wide.shape[0]
    for peer in range(PEERS):
        for turn in range(turns):
            lanes = slices_ref[peer, :, turn * LANES : (turn + 1) * LANES]
            wide[turn, peer * stride : peer * stride + needed, :] = lanes.astype(jnp.float32)

    def spread(group, slot):
        at = pl.ds(group * slots + slot, PEERS, stride=stride)
        picked = jnp.concatenate([wide[turn, at, :] for turn in range(turns)], axis=0).astype(slices_ref.dtype)
        row = jnp.where(slot < count_ref[group], row_ref[group, slot], 2)
        none = jnp.zeros_like(picked)
        return jnp.concatenate([jnp.where(row == 0, picked, none), jnp.where(row == 1, picked, none)], axis=1)

    total = None
    for group in range(groups):
        for first in range(0, slots, RUN):
            run = range(first, first + RUN)
            tiles = jnp.concatenate([tiles_ref[group, slot] for slot in run], axis=1)
            picked = jnp.concatenate([spread(group, slot) for slot in run], axis=0)
            product = jnp.dot(tiles, picked, preferred_element_type=jnp.float32)
            total = product if total is None else total + product

    width = total.shape[1] // 2
    aggregated = jnp.concatenate([total[:, :width], total[:, width:]], axis=0).astype(jnp.bfloat16)
    pre = jnp.dot(aggregated, weight_ref[...], preferred_element_type=jnp.float32) + bias_ref[...]
    result, derive = gelu_parts(pre)
    hidden_ref[...] = result.astype(jnp.bfloat16)
    slope = cotangent_ref[...].astype(jnp.float32) * derive
    outs = slope.shape[1]
    grad_ref[:, :outs] = lax.dot_general(
        aggregated, slope.astype(jnp.bfloat16), (((0,), (0,)), ((), ())), preferred_element_type=jnp.float32
    )
    bias_part = jnp.sum(slope, axis=0, keepdims=True)
    at = lax.broadcasted_iota(jnp.int32, (width, outs - width), 0)
    last = jnp.where(at == 1, bias_part[:, width:], 0.0)
    grad_ref[:, outs:] = jnp.where(at == 0, bias_part[:, :width], last)


def layer(rows, counts, tiles, slices, weight, bias, cotangent):
    nodes, out_width = cotangent.shape
    width = weight.shape[0]
    vmem = pl.BlockSpec(memory_space=pltpu.VMEM)
    smem = pl.BlockSpec(memory_space=pltpu.SMEM)
    return pl.pallas_call(
        layer_kernel,
        out_shape=(
            jax.ShapeDtypeStruct((nodes, out_width), jnp.bfloat16),
            jax.ShapeDtypeStruct((width, out_width + width), jnp.float32),
        ),
        in_specs=[smem, smem, vmem, vmem, vmem, vmem, vmem],
        out_specs=(vmem, vmem),
        scratch_shapes=[
            pltpu.VMEM((slices.shape[2] // LANES, PEERS * (slices.shape[1] + 1), LANES), jnp.float32),
        ],
        compiler_params=pltpu.CompilerParams(vmem_limit_bytes=32 * 1024 * 1024),
        name="layer",
    )(rows, counts, tiles, slices, weight, bias.reshape(1, -1), cotangent)


def sum_over_devices(grad):
    group = ('zlo', 'core', 'x', 'zhi', 'y')
    size = math.prod(SIZE[axis] for axis in group)
    rows = grad.reshape(size, -1, grad.shape[1])
    total = jnp.sum(lax.all_to_all(rows, group, 0, 0), axis=0)
    shared = lax.all_to_all(jnp.broadcast_to(total[None], rows.shape), group, 0, 0)
    return shared.reshape(grad.shape)


def stage_kernel(features_ref, cols_ref, features_out, cols_out):
    features_out[...] = features_ref[...]
    groups, slots = cols_ref.shape
    team = lax.broadcasted_iota(jnp.int32, (groups, slots), 0)
    need = (team * PANEL + cols_ref[...]).astype(jnp.float32)
    row = jnp.zeros((1, LANES), jnp.float32)
    for group in range(groups):
        at = lax.broadcasted_iota(jnp.int32, (slots, LANES), 1)
        own = lax.broadcasted_iota(jnp.int32, (slots, LANES), 0) + group * slots
        put = jnp.where(at == own, 1.0, 0.0)
        row += jnp.dot(need[group : group + 1], put, preferred_element_type=jnp.float32)
    cols_out[...] = row.astype(jnp.bfloat16)


def stage(features, cols):
    vmem = pl.BlockSpec(memory_space=pltpu.VMEM)
    return pl.pallas_call(
        stage_kernel,
        out_shape=(
            pltpu.VMEM(features.shape, features.dtype),
            pltpu.VMEM((1, LANES), jnp.bfloat16),
        ),
        in_specs=[vmem, vmem],
        out_specs=(vmem, vmem),
        name="stage",
    )(features, cols)


def local(features, tile_values, tile_row, tile_col, tile_count, weight, bias, cotangent):
    groups, slots, block, _ = tile_values.shape
    width = features.shape[1]
    turns = block // PEERS
    needed = groups * slots

    features, need = stage(features, tile_col)
    need = need.reshape(width)

    mine = features.reshape(-1, turns, PEERS, width).transpose(2, 0, 1, 3).reshape(PEERS, -1, turns * width)
    grid = [SIZE[axis] for axis in AXES]
    once = [1 if axis in ALIKE else SIZE[axis] for axis in AXES]
    copies = [SIZE[axis] if axis in ALIKE else 1 for axis in AXES]
    near = jnp.ones(copies + [1, 1], need.dtype)
    for axis in ALIKE:
        at = lax.broadcasted_iota(jnp.int32, near.shape, AXES.index(axis))
        near = jnp.where(at == lax.axis_index(axis), near, 0)
    rows = jnp.broadcast_to(mine.reshape(once + list(mine.shape[1:])), grid + list(mine.shape[1:]))
    lists = jnp.broadcast_to(need * near, grid + [mine.shape[1], width])
    sent = jnp.concatenate([rows, lists], axis=len(grid) + 1)
    dealt = lax.all_to_all(sent.reshape((-1,) + sent.shape[len(grid) :]), AXES, 0, 0)
    table = dealt[:, :, : turns * width].reshape(-1, turns * width)
    lists = dealt[:, 0, turns * width : turns * width + needed].reshape(grid + [needed])
    for axis in ALIKE:
        lists = jnp.max(lists, axis=AXES.index(axis), keepdims=True)
    wanted = lists.reshape(PEERS, needed).astype(jnp.int32).T

    slices = lax.all_to_all(pick_slices(wanted, table), DEAL, 0, 0)

    hidden, grad = layer(tile_row, tile_count, tile_values, slices, weight, bias, cotangent)
    summed = sum_over_devices(grad)
    return (hidden, summed[:, : bias.shape[0]], summed[:2, bias.shape[0] :].reshape(bias.shape))


def solution(mesh):
    fine = Mesh(mesh.devices.reshape(AXIS_SIZES), AXES)
    nodes = P(AXES)
    in_specs = (nodes, nodes, nodes, nodes, nodes, P(), P(), nodes)
    return jax.shard_map(
        local, mesh=fine, in_specs=in_specs, out_specs=(nodes, P(), P()), check_vma=False
    )
```

```python
import math

import jax
import jax.numpy as jnp
from jax import lax
from jax.experimental import pallas as pl
from jax.experimental.pallas import tpu as pltpu
from jax.sharding import Mesh, PartitionSpec as P

AXES = ("zlo", "core", "x", "zhi", "y")
AXIS_SIZES = (2, 2, 4, 2, 4)
SIZE = dict(zip(AXES, AXIS_SIZES))
ALIKE = ("zhi",)
DEAL = tuple(axis for axis in AXES if axis not in ALIKE)
PEERS = math.prod(SIZE[axis] for axis in DEAL)
SPAN = 8
RUN = 6
LANES = 128
PANEL = 2 * math.prod(AXIS_SIZES) // 4


def pick_kernel(need_ref, table_ref, out_ref):
    table = table_ref[...]
    need = need_ref[...]
    slots, span = need.shape[0], SPAN
    blocks = lax.broadcasted_iota(jnp.int32, (slots, table.shape[0]), 1)
    for run in range(PEERS // span):
        hot = [
            jnp.where(blocks == need[:, peer : peer + 1], 1.0, 0.0).astype(table.dtype)
            for peer in range(run * span, (run + 1) * span)
        ]
        rows = jnp.dot(jnp.concatenate(hot, axis=0), table, preferred_element_type=jnp.float32)
        out_ref[run * span : (run + 1) * span] = rows.astype(table.dtype).reshape(span, slots, table.shape[1])


def pick_slices(need, table):
    vmem = pl.BlockSpec(memory_space=pltpu.VMEM)
    shape = (PEERS, need.shape[0], table.shape[1])
    return pl.pallas_call(
        pick_kernel,
        out_shape=jax.ShapeDtypeStruct(shape, table.dtype),
        in_specs=[vmem] * 2,
        out_specs=vmem,
        compiler_params=pltpu.CompilerParams(vmem_limit_bytes=32 * 1024 * 1024),
        name="pick_slices",
    )(need, table)


def gelu_parts(values):
    gelu_coef = 0.7978845608
    tangent_h = jnp.tanh(gelu_coef * (values + 0.044715 * values * values * values))
    result = 0.5 * values * (1.0 + tangent_h)
    derive = 0.5 * (1.0 + tangent_h) + 0.5 * values * (1.0 - tangent_h * tangent_h) * gelu_coef * (
        1.0 + 3.0 * 0.044715 * values * values
    )
    return (result, derive)


def layer_kernel(
    row_ref, count_ref, tiles_ref, slices_ref, weight_ref, bias_ref, cotangent_ref, hidden_ref, grad_ref, wide
):
    groups, slots = tiles_ref.shape[:2]

    needed, stride = groups * slots, wide.shape[1] // PEERS
    turns = wide.shape[0]
    for peer in range(PEERS):
        for turn in range(turns):
            lanes = slices_ref[peer, :, turn * LANES : (turn + 1) * LANES]
            wide[turn, peer * stride : peer * stride + needed, :] = lanes.astype(jnp.float32)

    def spread(group, slot):
        at = pl.ds(group * slots + slot, PEERS, stride=stride)
        picked = jnp.concatenate([wide[turn, at, :] for turn in range(turns)], axis=0).astype(slices_ref.dtype)
        row = jnp.where(slot < count_ref[group], row_ref[group, slot], 2)
        none = jnp.zeros_like(picked)
        return jnp.concatenate([jnp.where(row == 0, picked, none), jnp.where(row == 1, picked, none)], axis=1)

    total = None
    for group in range(groups):
        for first in range(0, slots, RUN):
            run = range(first, first + RUN)
            tiles = jnp.concatenate([tiles_ref[group, slot] for slot in run], axis=1)
            picked = jnp.concatenate([spread(group, slot) for slot in run], axis=0)
            product = jnp.dot(tiles, picked, preferred_element_type=jnp.float32)
            total = product if total is None else total + product

    width = total.shape[1] // 2
    aggregated = jnp.concatenate([total[:, :width], total[:, width:]], axis=0).astype(jnp.bfloat16)
    pre = jnp.dot(aggregated, weight_ref[...], preferred_element_type=jnp.float32) + bias_ref[...]
    result, derive = gelu_parts(pre)
    hidden_ref[...] = result.astype(jnp.bfloat16)
    slope = cotangent_ref[...].astype(jnp.float32) * derive
    outs = slope.shape[1]
    grad_ref[:, :outs] = lax.dot_general(
        aggregated, slope.astype(jnp.bfloat16), (((0,), (0,)), ((), ())), preferred_element_type=jnp.float32
    )
    bias_part = jnp.sum(slope, axis=0, keepdims=True)
    at = lax.broadcasted_iota(jnp.int32, (width, outs - width), 0)
    last = jnp.where(at == 1, bias_part[:, width:], 0.0)
    grad_ref[:, outs:] = jnp.where(at == 0, bias_part[:, :width], last)


def layer(rows, counts, tiles, slices, weight, bias, cotangent):
    nodes, out_width = cotangent.shape
    width = weight.shape[0]
    vmem = pl.BlockSpec(memory_space=pltpu.VMEM)
    smem = pl.BlockSpec(memory_space=pltpu.SMEM)
    return pl.pallas_call(
        layer_kernel,
        out_shape=(
            jax.ShapeDtypeStruct((nodes, out_width), jnp.bfloat16),
            jax.ShapeDtypeStruct((width, out_width + width), jnp.float32),
        ),
        in_specs=[smem, smem, vmem, vmem, vmem, vmem, vmem],
        out_specs=(vmem, vmem),
        scratch_shapes=[
            pltpu.VMEM((slices.shape[2] // LANES, PEERS * (slices.shape[1] + 1), LANES), jnp.float32),
        ],
        compiler_params=pltpu.CompilerParams(vmem_limit_bytes=32 * 1024 * 1024),
        name="layer",
    )(rows, counts, tiles, slices, weight, bias.reshape(1, -1), cotangent)


def sum_over_devices(grad):
    group = ('zlo', 'core', 'x', 'zhi', 'y')
    size = math.prod(SIZE[axis] for axis in group)
    rows = grad.reshape(size, -1, grad.shape[1])
    total = jnp.sum(lax.all_to_all(rows, group, 0, 0), axis=0)
    shared = lax.all_to_all(jnp.broadcast_to(total[None], rows.shape), group, 0, 0)
    return shared.reshape(grad.shape)


def stage_kernel(at_ref, features_ref, cols_ref, features_out, cols_out):
    features_out[...] = features_ref[...]
    groups, slots = cols_ref.shape
    team = lax.broadcasted_iota(jnp.int32, (groups, slots), 0)
    need = (team * PANEL + cols_ref[...]).astype(jnp.float32)
    row = jnp.zeros((1, LANES), jnp.float32)
    for group in range(groups):
        at = lax.broadcasted_iota(jnp.int32, (slots, LANES), 1)
        own = lax.broadcasted_iota(jnp.int32, (slots, LANES), 0) + group * slots
        put = jnp.where(at == own, 1.0, 0.0)
        row += jnp.dot(need[group : group + 1], put, preferred_element_type=jnp.float32)
    place = lax.broadcasted_iota(jnp.int32, cols_out.shape, 0)
    cols_out[...] = jnp.where(place == at_ref[0], row, 0.0).astype(jnp.bfloat16)


def stage(at, features, cols):
    vmem = pl.BlockSpec(memory_space=pltpu.VMEM)
    return pl.pallas_call(
        stage_kernel,
        out_shape=(
            pltpu.VMEM(features.shape, features.dtype),
            pltpu.VMEM((SIZE[ALIKE[0]], LANES), jnp.bfloat16),
        ),
        in_specs=[pl.BlockSpec(memory_space=pltpu.SMEM), vmem, vmem],
        out_specs=(vmem, vmem),
        name="stage",
    )(at, features, cols)


def local(features, tile_values, tile_row, tile_col, tile_count, weight, bias, cotangent):
    groups, slots, block, _ = tile_values.shape
    width = features.shape[1]
    turns = block // PEERS
    needed = groups * slots

    features, need = stage(lax.axis_index(ALIKE[0]).reshape(1), features, tile_col)

    mine = features.reshape(-1, turns, PEERS, width).transpose(2, 0, 1, 3).reshape(PEERS, -1, turns * width)
    grid = [SIZE[axis] for axis in AXES]
    once = [1 if axis in ALIKE else SIZE[axis] for axis in AXES]
    copies = [SIZE[axis] if axis in ALIKE else 1 for axis in AXES]
    rows = jnp.broadcast_to(mine.reshape(once + list(mine.shape[1:])), grid + list(mine.shape[1:]))
    lists = jnp.broadcast_to(need.reshape(copies + [1, width]), grid + [mine.shape[1], width])
    sent = jnp.concatenate([rows, lists], axis=len(grid) + 1)
    dealt = lax.all_to_all(sent.reshape((-1,) + sent.shape[len(grid) :]), AXES, 0, 0)
    table = dealt[:, :, : turns * width].reshape(-1, turns * width)
    lists = dealt[:, 0, turns * width : turns * width + needed].reshape(grid + [needed])
    for axis in ALIKE:
        lists = jnp.max(lists, axis=AXES.index(axis), keepdims=True)
    wanted = lists.reshape(PEERS, needed).astype(jnp.int32).T

    slices = lax.all_to_all(pick_slices(wanted, table), DEAL, 0, 0)

    hidden, grad = layer(tile_row, tile_count, tile_values, slices, weight, bias, cotangent)
    summed = sum_over_devices(grad)
    return (hidden, summed[:, : bias.shape[0]], summed[:2, bias.shape[0] :].reshape(bias.shape))


def solution(mesh):
    fine = Mesh(mesh.devices.reshape(AXIS_SIZES), AXES)
    nodes = P(AXES)
    in_specs = (nodes, nodes, nodes, nodes, nodes, P(), P(), nodes)
    return jax.shard_map(
        local, mesh=fine, in_specs=in_specs, out_specs=(nodes, P(), P()), check_vma=False
    )
```

```python
import math

import jax
import jax.numpy as jnp
from jax import lax
from jax.experimental import pallas as pl
from jax.experimental.pallas import tpu as pltpu
from jax.sharding import Mesh, PartitionSpec as P

AXES = ("zlo", "core", "x", "zhi", "y")
AXIS_SIZES = (2, 2, 4, 2, 4)
SIZE = dict(zip(AXES, AXIS_SIZES))
ALIKE = ("zhi",)
DEAL = tuple(axis for axis in AXES if axis not in ALIKE)
PEERS = math.prod(SIZE[axis] for axis in DEAL)
SPAN = 32
RUN = 12
LANES = 128
PANEL = 2 * math.prod(AXIS_SIZES) // 4


def pick_kernel(need_ref, table_ref, out_ref):
    table = table_ref[...]
    need = need_ref[...]
    slots, span = need.shape[0], SPAN
    blocks = lax.broadcasted_iota(jnp.int32, (slots, table.shape[0]), 1)
    for run in range(PEERS // span):
        hot = [
            jnp.where(blocks == need[:, peer : peer + 1], 1.0, 0.0).astype(table.dtype)
            for peer in range(run * span, (run + 1) * span)
        ]
        rows = jnp.dot(jnp.concatenate(hot, axis=0), table, preferred_element_type=jnp.float32)
        out_ref[run * span : (run + 1) * span] = rows.astype(table.dtype).reshape(span, slots, table.shape[1])


def pick_slices(need, table):
    vmem = pl.BlockSpec(memory_space=pltpu.VMEM)
    shape = (PEERS, need.shape[0], table.shape[1])
    return pl.pallas_call(
        pick_kernel,
        out_shape=jax.ShapeDtypeStruct(shape, table.dtype),
        in_specs=[vmem] * 2,
        out_specs=vmem,
        compiler_params=pltpu.CompilerParams(vmem_limit_bytes=32 * 1024 * 1024),
        name="pick_slices",
    )(need, table)


def gelu_parts(values):
    gelu_coef = 0.7978845608
    tangent_h = jnp.tanh(gelu_coef * (values + 0.044715 * values * values * values))
    result = 0.5 * values * (1.0 + tangent_h)
    derive = 0.5 * (1.0 + tangent_h) + 0.5 * values * (1.0 - tangent_h * tangent_h) * gelu_coef * (
        1.0 + 3.0 * 0.044715 * values * values
    )
    return (result, derive)


def layer_kernel(
    row_ref, count_ref, tiles_ref, slices_ref, weight_ref, bias_ref, cotangent_ref, hidden_ref, grad_ref, wide
):
    groups, slots = tiles_ref.shape[:2]

    needed, stride = groups * slots, wide.shape[1] // PEERS
    turns = wide.shape[0]
    for peer in range(PEERS):
        for turn in range(turns):
            lanes = slices_ref[peer, :, turn * LANES : (turn + 1) * LANES]
            wide[turn, peer * stride : peer * stride + needed, :] = lanes.astype(jnp.float32)

    def spread(group, slot):
        at = pl.ds(group * slots + slot, PEERS, stride=stride)
        picked = jnp.concatenate([wide[turn, at, :] for turn in range(turns)], axis=0).astype(slices_ref.dtype)
        row = jnp.where(slot < count_ref[group], row_ref[group, slot], 2)
        none = jnp.zeros_like(picked)
        return jnp.concatenate([jnp.where(row == 0, picked, none), jnp.where(row == 1, picked, none)], axis=1)

    total = None
    for group in range(groups):
        for first in range(0, slots, RUN):
            run = range(first, first + RUN)
            tiles = jnp.concatenate([tiles_ref[group, slot] for slot in run], axis=1)
            picked = jnp.concatenate([spread(group, slot) for slot in run], axis=0)
            product = jnp.dot(tiles, picked, preferred_element_type=jnp.float32)
            total = product if total is None else total + product

    width = total.shape[1] // 2
    aggregated = jnp.concatenate([total[:, :width], total[:, width:]], axis=0).astype(jnp.bfloat16)
    pre = jnp.dot(aggregated, weight_ref[...], preferred_element_type=jnp.float32) + bias_ref[...]
    result, derive = gelu_parts(pre)
    hidden_ref[...] = result.astype(jnp.bfloat16)
    slope = cotangent_ref[...].astype(jnp.float32) * derive
    outs = slope.shape[1]
    grad_ref[:, :outs] = lax.dot_general(
        aggregated, slope.astype(jnp.bfloat16), (((0,), (0,)), ((), ())), preferred_element_type=jnp.float32
    )
    bias_part = jnp.sum(slope, axis=0, keepdims=True)
    at = lax.broadcasted_iota(jnp.int32, (width, outs - width), 0)
    last = jnp.where(at == 1, bias_part[:, width:], 0.0)
    grad_ref[:, outs:] = jnp.where(at == 0, bias_part[:, :width], last)


def layer(rows, counts, tiles, slices, weight, bias, cotangent):
    nodes, out_width = cotangent.shape
    width = weight.shape[0]
    vmem = pl.BlockSpec(memory_space=pltpu.VMEM)
    smem = pl.BlockSpec(memory_space=pltpu.SMEM)
    return pl.pallas_call(
        layer_kernel,
        out_shape=(
            jax.ShapeDtypeStruct((nodes, out_width), jnp.bfloat16),
            jax.ShapeDtypeStruct((width, out_width + width), jnp.float32),
        ),
        in_specs=[smem, smem, vmem, vmem, vmem, vmem, vmem],
        out_specs=(vmem, vmem),
        scratch_shapes=[
            pltpu.VMEM((slices.shape[2] // LANES, PEERS * (slices.shape[1] + 1), LANES), jnp.float32),
        ],
        compiler_params=pltpu.CompilerParams(vmem_limit_bytes=32 * 1024 * 1024),
        name="layer",
    )(rows, counts, tiles, slices, weight, bias.reshape(1, -1), cotangent)


def sum_over_devices(grad):
    group = ('zlo', 'core', 'x', 'zhi', 'y')
    size = math.prod(SIZE[axis] for axis in group)
    rows = grad.reshape(size, -1, grad.shape[1])
    total = jnp.sum(lax.all_to_all(rows, group, 0, 0), axis=0)
    shared = lax.all_to_all(jnp.broadcast_to(total[None], rows.shape), group, 0, 0)
    return shared.reshape(grad.shape)


def stage_kernel(at_ref, features_ref, cols_ref, features_out, cols_out):
    features_out[...] = features_ref[...]
    groups, slots = cols_ref.shape
    team = lax.broadcasted_iota(jnp.int32, (groups, slots), 0)
    need = (team * PANEL + cols_ref[...]).astype(jnp.float32)
    row = jnp.zeros((1, LANES), jnp.float32)
    for group in range(groups):
        at = lax.broadcasted_iota(jnp.int32, (slots, LANES), 1)
        own = lax.broadcasted_iota(jnp.int32, (slots, LANES), 0) + group * slots
        put = jnp.where(at == own, 1.0, 0.0)
        row += jnp.dot(need[group : group + 1], put, preferred_element_type=jnp.float32)
    place = lax.broadcasted_iota(jnp.int32, cols_out.shape, 0)
    cols_out[...] = jnp.where(place == at_ref[0], row, 0.0).astype(jnp.bfloat16)


def stage(at, features, cols):
    vmem = pl.BlockSpec(memory_space=pltpu.VMEM)
    return pl.pallas_call(
        stage_kernel,
        out_shape=(
            pltpu.VMEM(features.shape, features.dtype),
            pltpu.VMEM((SIZE[ALIKE[0]], LANES), jnp.bfloat16),
        ),
        in_specs=[pl.BlockSpec(memory_space=pltpu.SMEM), vmem, vmem],
        out_specs=(vmem, vmem),
        name="stage",
    )(at, features, cols)


def local(features, tile_values, tile_row, tile_col, tile_count, weight, bias, cotangent):
    groups, slots, block, _ = tile_values.shape
    width = features.shape[1]
    turns = block // PEERS
    needed = groups * slots

    features, need = stage(lax.axis_index(ALIKE[0]).reshape(1), features, tile_col)

    mine = features.reshape(-1, turns, PEERS, width).transpose(2, 0, 1, 3).reshape(PEERS, -1, turns * width)
    grid = [SIZE[axis] for axis in AXES]
    once = [1 if axis in ALIKE else SIZE[axis] for axis in AXES]
    copies = [SIZE[axis] if axis in ALIKE else 1 for axis in AXES]
    rows = jnp.broadcast_to(mine.reshape(once + list(mine.shape[1:])), grid + list(mine.shape[1:]))
    lists = jnp.broadcast_to(need.reshape(copies + [1, width]), grid + [mine.shape[1], width])
    sent = jnp.concatenate([rows, lists], axis=len(grid) + 1)
    dealt = lax.all_to_all(sent.reshape((-1,) + sent.shape[len(grid) :]), AXES, 0, 0)
    table = dealt[:, :, : turns * width].reshape(-1, turns * width)
    lists = dealt[:, 0, turns * width : turns * width + needed].reshape(grid + [needed])
    for axis in ALIKE:
        lists = jnp.max(lists, axis=AXES.index(axis), keepdims=True)
    wanted = lists.reshape(PEERS, needed).astype(jnp.int32).T

    slices = lax.all_to_all(pick_slices(wanted, table), DEAL, 0, 0)

    hidden, grad = layer(tile_row, tile_count, tile_values, slices, weight, bias, cotangent)
    summed = sum_over_devices(grad)
    return (hidden, summed[:, : bias.shape[0]], summed[:2, bias.shape[0] :].reshape(bias.shape))


def solution(mesh):
    fine = Mesh(mesh.devices.reshape(AXIS_SIZES), AXES)
    nodes = P(AXES)
    in_specs = (nodes, nodes, nodes, nodes, nodes, P(), P(), nodes)
    return jax.shard_map(
        local, mesh=fine, in_specs=in_specs, out_specs=(nodes, P(), P()), check_vma=False
    )
```
